32 devices in a mesh: pipe: 2 (over core), row: 4 (over y, x), col: 4 (over z).
Axes of the slice: x: 2, y: 2, z: 4, core: 2. Of those that a mesh axis runs over, the one named last changes fastest.
Arguments:
- section_input: float32 [2, 4096, 768], P(None, ('row', 'col')), may hold values from -6 to 6
- cotangent: float32 [2, 4096, 768], P(None, ('row', 'col')), may hold values from -6 to 6
- qkv_weight: bfloat16 [2, 768, 2304], P('pipe', ('row', 'col')), may hold values from -0.21875 to 0.21875
- out_weight: bfloat16 [2, 768, 768], P('pipe', ('row', 'col')), may hold values from -1 to 1
- router_weight: bfloat16 [2, 768, 64], P('pipe', ('row', 'col')), may hold values from -0.15625 to 0.15625
- gain_attn: bfloat16 [2, 768], P('pipe', ('row', 'col')), may hold values from 0.25 to 1.75
- gain_moe: bfloat16 [2, 768], P('pipe', ('row', 'col')), may hold values from 0.25 to 1.75
- rel_bias: bfloat16 [2, 384], P('pipe', ('row', 'col')), may hold values from -6 to 6
- expert_in: bfloat16 [2, 64, 768, 3072], P('pipe', 'row', None, 'col'), may hold values from -0.21875 to 0.21875
- expert_out: bfloat16 [2, 64, 3072, 768], P('pipe', 'row', 'col'), may hold values from -0.21875 to 0.21875
- routes: int32 [2, 2, 4096, 2], P('pipe', None, ('row', 'col')), may hold values from 0 to 63, all different within a row; in each aligned block of 256 rows (0 to 255, 256 to 511, ..., all dimensions but the last counted through in order) at most 12 rows name the same one
- doc_ids: int32 [2, 4096], P(None, 'row'), may hold values from 0 to 3, as said below
- buckets: int32 [1024], replicated, may hold values from 0 to 31, never falling along the last dimension, each value on 1 to 64 neighbouring positions
Outputs:
- section_outputs: float32 [2, 2, 4096, 768], P('pipe', None, ('row', 'col'))
- input_grads: float32 [2, 2, 4096, 768], P('pipe', None, ('row', 'col'))
- grad_qkv_weight: float32 [2, 768, 2304], P('pipe', ('row', 'col'))
- grad_out_weight: float32 [2, 768, 768], P('pipe', ('row', 'col'))
- grad_router_weight: float32 [2, 768, 64], P('pipe', ('row', 'col'))
- grad_gain_attn: float32 [2, 768], P('pipe', ('row', 'col'))
- grad_gain_moe: float32 [2, 768], P('pipe', ('row', 'col'))
- grad_rel_bias: float32 [2, 384], P('pipe', ('row', 'col'))
- grad_expert_in: float32 [2, 64, 768, 3072], P('pipe', 'row', None, 'col')
- grad_expert_out: float32 [2, 64, 3072, 768], P('pipe', 'row', 'col')
The draws below stay inside these ranges and needn't reach their ends.
Inputs may be any that keep to these rules, and one draw needn't show every extreme that they name: `routes`: each token names 2 different experts; in each aligned block of 256 rows (the tokens of one device, sections and micro-batches in order) no expert is named more than 12 times, a bound that some block reaches. `doc_ids`: numbers the documents of each sequence from 0 at its first position, never falling and rising by at most one from a position to the next; for every index of row one of its 2 sequences is a single document. `buckets`: never falling with the distance; every bucket is used.
All inputs are finite; a program needn't handle non-finite values.
Results may differ from the reference program's by a relative error of at most 0.025.
Values may be sent and summed in bfloat16 or wider, within the bound.
No kernel may reach another device: no remote copies, remote signals or barrier semaphores. Data moves between devices by JAX's collectives and lax.ppermute only.
A program may use at most 576 MiB of HBM per device.

```python
import math
import jax
import jax.numpy as jnp
import numpy as np
from jax import lax

D = 768
HEADS = 12
HEAD_DIM = 64
FF = 3072
EXPERTS = 64
TOP = 2
NBUCKET = 32
SEQ = 1024
SEQS_ROW = 1
MB = 2
PIECE = 256
TOK_DEV = 256
TOKENS = 4096
CAP = 12
N_PIPE = 2


def draw_doc_ids(key, part):
    key = jax.random.fold_in(key, 7)
    groups = TOKENS // (SEQS_ROW * SEQ)
    first_key, second_key = jax.random.split(key)
    starts = jax.random.randint(first_key, (MB, groups, SEQS_ROW, SEQ), 0, SEQ // 8) == 0
    chosen = jax.random.randint(second_key, (groups,), 0, MB * SEQS_ROW)
    number = jnp.arange(MB, dtype=jnp.int32)[:, None, None] * SEQS_ROW + jnp.arange(SEQS_ROW, dtype=jnp.int32)[None, None, :]
    single = number == chosen[None, :, None]
    places = jnp.arange(SEQ, dtype=jnp.int32)[None, None, None, :]
    after_first = places > 0
    closing = places >= SEQ - 3
    boundary = ((starts | closing) & after_first & jnp.logical_not(single)[:, :, :, None]).astype(jnp.int32)
    numbers = jnp.minimum(jnp.cumsum(boundary, axis=3), 3).astype(jnp.int32)
    numbers = numbers.reshape(MB, groups, SEQS_ROW, SEQ // PIECE, PIECE)
    return jnp.transpose(numbers, (0, 1, 3, 2, 4)).reshape(MB, TOKENS)


def strengthened(values, rng, source, target, blocks, factor):
    def block_of(dim):
        return (jnp.arange(values.shape[dim]) // (values.shape[dim] // blocks)).reshape((-1,) + (1,) * (values.ndim - 1 - dim))

    near = jax.random.permutation(rng, blocks)[block_of(target)]
    second = (block_of(target) + blocks // 2) % blocks
    return jnp.where((block_of(source) == near) | (block_of(source) == second), factor * values, values)


def block_scale(own_key, dims, pieces, smallest, high):
    def one(axis_at, parts):
        steps = jax.random.uniform(jax.random.fold_in(jax.random.fold_in(own_key, 6), axis_at), (parts,), jnp.float32, smallest / len(pieces), high / len(pieces))
        return jnp.repeat(jnp.exp(steps), dims[axis_at] // parts).reshape((-1,) + (1,) * (len(dims) - axis_at - 1))

    level = one(*pieces[0])
    for cut in pieces[1:]:
        level = level * one(*cut)
    return level


def length_profile(count, total, most, skew):
    loads = [(1 << 20) // math.isqrt(rank ** skew) + 1 for rank in range(2, count + 1)]
    surplus, counts = total - most - (count - 1), [1] * (count - 1)
    while surplus > 0:
        candidates = [i for i in range(count - 1) if counts[i] < most]
        mass, left = sum([loads[i] for i in candidates]), surplus
        for i in candidates:
            addition = min(most - counts[i], max(1, left * loads[i] // mass), surplus)
            counts[i] = counts[i] + addition
            surplus = surplus - addition
    return np.array([most] + counts)


def uneven_parts(rng, amount, total, limit, slope):
    if amount == 2:
        one = jax.random.randint(rng, (), max(1, total - limit), min(limit, total - 1) + 1)
        return jnp.stack([one, total - one])
    tallies = jnp.asarray(length_profile(amount, total, limit, slope), jnp.int32)
    pairs = (amount - 1) // 2
    giver, receiver = tallies[1:1 + 2 * pairs:2], tallies[2:2 + 2 * pairs:2]
    slack = jnp.minimum(giver - 1, limit - receiver)
    moved = jax.random.randint(jax.random.fold_in(rng, 1), (pairs,), 0, 1 << 20) % (slack + 1)
    tallies = tallies.at[1:1 + 2 * pairs:2].set(giver - moved).at[2:2 + 2 * pairs:2].set(receiver + moved)
    return tallies[jax.random.permutation(jax.random.fold_in(rng, 2), amount)]


def deal_out(key, own, number, rows, count, top, limit, lean):
    sequence = jax.random.permutation(key, count)
    heavy_load, common = portions_of(count, rows * top, limit, lean, True), portions_of(count, rows * top, limit, lean, False)
    places = jnp.arange(count)

    def named(tallies, rotation):
        used = int((tallies > 0).sum())
        fixed = max(1, used // 4)
        passed = fixed + (places - fixed + rotation * (used - fixed)) % max(1, count - fixed)
        return jnp.zeros((count,), jnp.int32).at[sequence[jnp.where(places < fixed, places, passed)]].set(jnp.asarray(tallies, jnp.int32))

    tallies = jnp.where(number % 4 == 0, named(heavy_load, number // 4), named(common, number - number // 4 - 1))
    mixed = jax.random.permutation(jax.random.fold_in(own, 3), count)
    source_of, sink = mixed[0:count // 2 * 2:2], mixed[1:count // 2 * 2:2]
    slack = jnp.minimum(tallies[source_of] - 1, limit - tallies[sink]) // 2
    slack = jnp.where((source_of == sequence[0]) | (sink == sequence[0]) | (tallies[sink] == 0), 0, jnp.maximum(slack, 0))
    passed = jax.random.randint(jax.random.fold_in(own, 4), (count // 2,), 0, 1 << 20) % (slack + 1)
    tallies = tallies.at[source_of].add(-passed).at[sink].add(passed)
    items = jnp.searchsorted(jnp.cumsum(tallies), jnp.arange(rows * top), side="right").astype(jnp.int32)
    listing = items.reshape(top, rows).T
    listing = listing[jax.random.permutation(jax.random.fold_in(own, 1), rows)]
    rotation = jax.random.randint(jax.random.fold_in(own, 2), (rows, 1), 0, top)
    return jnp.take_along_axis(listing, (jnp.arange(top)[None, :] + rotation) % top, axis=1)


def portions_of(amount, total, limit, slope, full):
    weights = [(1 << 20) // math.isqrt(rank ** slope) + 1 for rank in range(1, amount + 1)]
    largest = limit if full else min(limit, max(-(-total // amount), total * weights[0] // sum(weights)))
    least = 1 if total - largest >= amount - 1 else 0
    counts, surplus = [largest] + [least] * (amount - 1), total - largest - least * (amount - 1)
    while surplus > 0:
        candidates = [i for i in range(1, amount) if counts[i] < largest] or [i for i in range(1, amount) if counts[i] < limit]
        pool, left = sum([weights[i] for i in candidates]), surplus
        for i in candidates:
            extra = min(limit - counts[i], max(1, left * weights[i] // pool), surplus)
            counts[i] = counts[i] + extra
            surplus = surplus - extra
    return np.array(counts)


def gaussian(own_key, dims, deviation, bound, cuts=(), held_as=jnp.bfloat16):
    entries = deviation * jax.random.normal(own_key, dims, jnp.float32)
    if cuts:
        entries = entries * block_scale(own_key, dims, cuts, -0.22, 0.18)
    return jnp.clip(entries, -bound, bound).astype(held_as)


def gaussian_with(own_key, shape, scale, bound, pieces, heavy, kind=jnp.bfloat16):
    drawn = scale * jax.random.normal(own_key, shape, jnp.float32)
    if pieces:
        drawn = drawn * block_scale(own_key, shape, pieces, -0.22, 0.18)
    return jnp.clip(strengthened(drawn, jax.random.fold_in(own_key, 3), *heavy), -bound, bound).astype(kind)


def setup_inputs(seed: int = 0) -> dict:
    streams_of = jax.random.split(jax.random.key(seed), 14)
    section_input = gaussian_with(streams_of[0], (MB, TOKENS, D), 1.0, 6.0, ((1, 16),), (1, 2, 16, 2.0), jnp.float32)
    cotangent = gaussian_with(streams_of[1], (MB, TOKENS, D), 1.0, 6.0, ((1, 16),), (1, 2, 16, 2.0), jnp.float32)
    qkv_weight = gaussian(streams_of[2], (N_PIPE, D, 3 * D), D ** -0.5, 0.21875, ((0, 2), (1, 16)))
    out_weight = gaussian(streams_of[3], (N_PIPE, D, D), 32 ** -0.5, 1.0, ((0, 2), (1, 16)))
    router_weight = gaussian(streams_of[4], (N_PIPE, D, EXPERTS), 0.025, 0.15625, ((0, 2), (1, 16)))
    gain_attn = jnp.clip(1.0 + 0.15 * jax.random.normal(streams_of[5], (N_PIPE, D), jnp.float32), 0.25, 1.75).astype(jnp.bfloat16)
    gain_moe = jnp.clip(1.0 + 0.15 * jax.random.normal(streams_of[6], (N_PIPE, D), jnp.float32), 0.25, 1.75).astype(jnp.bfloat16)
    rel_bias = gaussian(streams_of[7], (N_PIPE, NBUCKET * HEADS), 1.0, 6.0, ((0, 2), (1, 16)))
    expert_in = gaussian(streams_of[8], (N_PIPE, EXPERTS, D, FF), D ** -0.5, 0.21875, ((0, 2), (1, 4), (3, 4)))
    expert_out = gaussian(streams_of[9], (N_PIPE, EXPERTS, FF, D), (FF // 4) ** -0.5, 0.21875, ((0, 2), (1, 4), (2, 4)))
    routes_keys = jax.random.split(jax.random.fold_in(streams_of[10], 1), N_PIPE * MB * TOKENS // TOK_DEV)
    routes_turns = jax.random.permutation(jax.random.fold_in(streams_of[10], 3), N_PIPE * MB * TOKENS // TOK_DEV)
    routes = jax.vmap(lambda own, number: deal_out(jax.random.fold_in(streams_of[10], 2), own, number, TOK_DEV, EXPERTS, TOP, CAP, 1))(routes_keys, routes_turns).reshape((N_PIPE, MB, TOKENS, TOP))
    doc_ids = draw_doc_ids(jax.random.fold_in(streams_of[13], 71), 0)
    buckets = jnp.searchsorted(jnp.cumsum(uneven_parts(streams_of[12], NBUCKET, SEQ, 2 * SEQ // NBUCKET, 0)), jnp.arange(SEQ), side="right").astype(jnp.int32)
    return dict(section_input=section_input, cotangent=cotangent, qkv_weight=qkv_weight, out_weight=out_weight, router_weight=router_weight, gain_attn=gain_attn, gain_moe=gain_moe, rel_bias=rel_bias, expert_in=expert_in, expert_out=expert_out, routes=routes, doc_ids=doc_ids, buckets=buckets)


@jax.custom_vjp
def low(v):
    return lax.optimization_barrier(v.astype(jnp.bfloat16)).astype(jnp.float32)

@jax.custom_vjp
def low_back(v):
    return v

def low_keep(v):
    return (low(v), None)

def low_pass(kept, grad):
    return (grad,)

def back_keep(v):
    return (v, None)

def back_low(kept, grad):
    return (low(grad),)
low.defvjp(low_keep, low_pass)
low_back.defvjp(back_keep, back_low)
HIGH = lax.Precision.HIGHEST
EPS = 1e-06
MASKED = -1e+30

def matmul(factor, second):
    return jnp.dot(factor, second, precision=HIGH, preferred_element_type=jnp.float32)

def norm_scale(stream, norm_gain):
    return stream * lax.rsqrt(lax.optimization_barrier(jnp.mean(stream * stream, axis=-1, keepdims=True)) + EPS) * norm_gain

def to_sequences(values):
    trailing = values.shape[1:]
    groups = values.shape[0] // (SEQS_ROW * SEQ)
    values = values.reshape((groups, SEQ // PIECE, SEQS_ROW, PIECE) + trailing)
    values = jnp.swapaxes(values, 1, 2)
    return values.reshape((groups * SEQS_ROW, SEQ) + trailing)

def from_sequences(values):
    trailing = values.shape[2:]
    groups = values.shape[0] // SEQS_ROW
    values = values.reshape((groups, SEQS_ROW, SEQ // PIECE, PIECE) + trailing)
    values = jnp.swapaxes(values, 1, 2)
    return values.reshape((groups * SEQS_ROW * SEQ,) + trailing)

def attend_sequence(queries, key_rows, value_rows, documents, by_dist):
    raw_scores = low_back(jnp.einsum('qhd,khd->hqk', queries, key_rows, precision=HIGH))
    positions = jnp.arange(SEQ, dtype=jnp.int32)
    distance = positions[:, None] - positions[None, :]
    pos_bias = jnp.take(by_dist, jnp.clip(distance, 0, SEQ - 1), axis=1)
    scores = raw_scores * HEAD_DIM ** (-0.5) + pos_bias
    allowed = (distance >= 0) & (documents[:, None] == documents[None, :])
    scores = jnp.where(allowed[None], scores, MASKED)
    maxima = lax.optimization_barrier(jnp.max(scores, axis=-1, keepdims=True))
    weights = jnp.exp(scores - maxima)
    probability = low(weights / lax.optimization_barrier(jnp.sum(weights, axis=-1, keepdims=True)))
    return jnp.einsum('hqk,khd->qhd', probability, value_rows, precision=HIGH)

def expert_rows(rows_in, weight_in, weight_out):
    hidden = low_back(matmul(rows_in, weight_in))
    activated = low(jax.nn.gelu(hidden))
    return low_back(low(matmul(activated, weight_out)))

def section_layer(params, stream, routes, documents, buckets):
    qkv_weight, out_weight, router_weight, gain_attn, gain_moe, rel_bias, expert_in, expert_out = params
    tokens = stream.shape[0]
    normed_attn = low(norm_scale(stream, gain_attn))
    qkv = low_back(low(matmul(normed_attn, qkv_weight)))
    thirds = [to_sequences(qkv[:, i * D:(i + 1) * D]).reshape(-1, SEQ, HEADS, HEAD_DIM) for i in range(3)]
    by_dist = rel_bias.reshape(NBUCKET, HEADS)[buckets].T
    attend_fn = jax.checkpoint(lambda member: attend_sequence(member[0], member[1], member[2], member[3], by_dist))
    attended = lax.map(attend_fn, (thirds[0], thirds[1], thirds[2], to_sequences(documents)))
    mixed_low = low_back(low(from_sequences(attended.reshape(-1, SEQ, D))))
    after_attn = stream + low_back(matmul(mixed_low, out_weight))
    normed_moe = low(norm_scale(after_attn, gain_moe))
    logits = low_back(matmul(normed_moe, router_weight))
    chosen = jnp.take_along_axis(logits, routes, axis=1)
    chosen = jnp.exp(chosen - lax.optimization_barrier(jnp.max(chosen, axis=1, keepdims=True)))
    gate_weights = chosen / lax.optimization_barrier(jnp.sum(chosen, axis=1, keepdims=True))
    blocks = tokens // TOK_DEV
    flat_routes = routes.reshape(blocks, TOK_DEV * TOP)
    one_hot = (flat_routes[:, :, None] == jnp.arange(EXPERTS, dtype=jnp.int32)[None, None, :]).astype(jnp.int32)
    running = jnp.cumsum(one_hot, axis=1).astype(jnp.int32)
    slot_index = lax.optimization_barrier(jnp.sum((running - 1) * one_hot, axis=2)).astype(jnp.int32)
    destination = flat_routes * (blocks * CAP) + jnp.arange(blocks, dtype=jnp.int32)[:, None] * CAP + slot_index
    destination = destination.reshape(-1).astype(jnp.int32)
    token_rows = low_back(jnp.repeat(normed_moe, TOP, axis=0))
    buffer = jnp.zeros((EXPERTS * blocks * CAP, D), jnp.float32).at[destination].set(token_rows)
    expert_fn = jax.checkpoint(lambda member: expert_rows(member[0], member[1], member[2]))
    expert_outs = lax.map(expert_fn, (buffer.reshape(EXPERTS, blocks * CAP, D), expert_in, expert_out))
    returned = expert_outs.reshape(-1, D)[destination].reshape(tokens, TOP, D)
    return after_attn + lax.optimization_barrier(jnp.sum(gate_weights[:, :, None] * returned, axis=1))

def reference(section_input, cotangent, qkv_weight, out_weight, router_weight, gain_attn, gain_moe, rel_bias, expert_in, expert_out, routes, doc_ids, buckets):
    stacked = (qkv_weight, out_weight, router_weight, gain_attn, gain_moe, rel_bias, expert_in, expert_out)

    def section_params(section_number):
        return tuple((weight.astype(jnp.float32)[section_number] for weight in stacked))

    def section_run(section_number):

        def run_section(params, inputs):
            return jnp.stack([section_layer(params, inputs[m], routes[section_number, m], doc_ids[m], buckets) for m in range(MB)])
        return run_section
    out_one, back_one = jax.vjp(section_run(0), section_params(0), section_input.astype(jnp.float32))
    out_two, back_two = jax.vjp(section_run(1), section_params(1), out_one)
    grads_two, input_two = back_two(cotangent.astype(jnp.float32))
    grads_one, input_one = back_one(input_two)
    joined = [jnp.stack([former, latter]) for former, latter in zip(grads_one, grads_two)]
    return (jnp.stack([out_one, out_two]), jnp.stack([input_one, input_two]), joined[0], joined[1], joined[2], joined[3], joined[4], joined[5], joined[6], joined[7])
```

```python
import functools

import jax
import jax.numpy as jnp
from jax import lax
from jax.experimental import pallas as pl
from jax.experimental.pallas import tpu as pltpu
from jax.sharding import PartitionSpec as P

HEADS = 12
HEAD_DIM = 64
EXPERTS = 64
TOP = 2
NBUCKET = 32
LANES = 128

EPS = 1e-06
MASKED = -1e30
HIGH = lax.Precision.HIGHEST
BF = jnp.bfloat16
F32 = jnp.float32
VMEM_LIMIT = 56 * 1024 * 1024
SCORE_ROWS = 16
SMALL_ROWS = 16
GELU_C = 0.7978845608028654
GELU_A = 0.044715


def norm_scale(stream, norm_gain):
    return stream * lax.rsqrt(jnp.mean(stream * stream, axis=-1, keepdims=True) + EPS) * norm_gain


X_PAIRS = [(i, i ^ 1) for i in range(4)]
Y_PAIRS = [(i, i ^ 2) for i in range(4)]


def swap_pipe(value):
    return lax.ppermute(value, "pipe", [(0, 1), (1, 0)])


def shift_col(value, distance):
    count = lax.axis_size("col")
    return lax.ppermute(value, "col", [(i, (i + distance) % count) for i in range(count)])


def is_small(rows, cols):
    return rows == 4 and cols == 4


def block_order(rows, cols):
    row, col = lax.axis_index("row"), lax.axis_index("col")
    if not is_small(rows, cols):
        return jnp.arange(rows * cols, dtype=jnp.int32)
    steps = jnp.arange(cols, dtype=jnp.int32)
    flips = jnp.arange(rows, dtype=jnp.int32)
    source_col = (col - steps + cols) % cols
    source_row = row ^ flips
    return (source_row[None, :] * cols + source_col[:, None]).reshape(-1)


def gather_groups(block):
    cols = lax.axis_size("col")
    half = block.shape[1] // 2
    groups = []
    for step in range(cols):
        following = shift_col(block, 1) if step + 1 < cols else None
        from_x = lax.ppermute(block, "row", X_PAIRS)
        from_y = lax.ppermute(block, "row", Y_PAIRS)
        left = lax.ppermute(from_y[:, :half], "row", X_PAIRS)
        right = lax.ppermute(from_x[:, half:], "row", Y_PAIRS)
        groups.append((block, from_x, from_y, left, right))
        block = following
    return groups


def scatter_groups(groups):
    cols = lax.axis_size("col")
    total = None
    for step in range(cols - 1, -1, -1):
        own, for_x, for_y, left, right = groups[step]
        half = left.shape[1]
        left = lax.ppermute(left, "row", X_PAIRS)
        right = lax.ppermute(right, "row", Y_PAIRS)
        for_y = jnp.concatenate(
            [(for_y[:, :half].astype(F32) + left.astype(F32)).astype(BF), for_y[:, half:]], axis=1
        )
        for_x = jnp.concatenate(
            [for_x[:, :half], (for_x[:, half:].astype(F32) + right.astype(F32)).astype(BF)], axis=1
        )
        from_x = lax.ppermute(for_x, "row", X_PAIRS)
        from_y = lax.ppermute(for_y, "row", Y_PAIRS)
        summed = own.astype(F32) + from_x.astype(F32) + from_y.astype(F32)
        if step:
            summed = shift_col(summed.astype(BF), cols - step).astype(F32)
        total = summed if total is None else total + summed
    return total


def gather_absolute(block, order):
    rows, cols = lax.axis_size("row"), lax.axis_size("col")
    if not is_small(rows, cols):
        return lax.all_gather(block, ("row", "col"), axis=0)
    whole = jnp.zeros((rows * cols,) + block.shape, block.dtype)
    for step, (own, from_x, from_y, left, right) in enumerate(gather_groups(block)):
        across = jnp.concatenate([left, right], axis=1)
        for flip, value in enumerate((own, from_x, from_y, across)):
            whole = lax.dynamic_update_index_in_dim(whole, value, order[step * rows + flip], 0)
    return whole


def gather_tokens(block):
    if is_small(lax.axis_size("row"), lax.axis_size("col")):
        return gather_groups(block)
    return lax.all_gather(block, ("row", "col"), axis=0)


def scatter_tokens(parts):
    if is_small(lax.axis_size("row"), lax.axis_size("col")):
        return scatter_groups(parts)
    return lax.psum_scatter(parts, ("row", "col"), scatter_dimension=0, tiled=False).astype(F32)


def scatter_absolute(parts, order):
    rows, cols = lax.axis_size("row"), lax.axis_size("col")
    if not is_small(rows, cols):
        return lax.psum_scatter(parts, ("row", "col"), scatter_dimension=0, tiled=False).astype(F32)
    half = parts.shape[2] // 2
    groups = []
    for step in range(cols):
        own, for_x, for_y, across = [
            lax.dynamic_index_in_dim(parts, order[step * rows + flip], 0, keepdims=False)
            for flip in range(rows)
        ]
        groups.append((own, for_x, for_y, across[:, :half], across[:, half:]))
    return scatter_groups(groups)


def gather_sequence(block):
    rows, cols = lax.axis_size("row"), lax.axis_size("col")
    if not is_small(rows, cols):
        return lax.all_gather(block, "col", axis=0, tiled=True)
    col = lax.axis_index("col")
    count = block.shape[0]
    whole = jnp.zeros((cols * count, block.shape[1]), block.dtype)
    for step in range(cols):
        place = (col - step + cols) % cols * count
        whole = lax.dynamic_update_slice(whole, block, (place, jnp.zeros_like(place)))
        if step + 1 < cols:
            block = shift_col(block, 1)
    return whole


def scatter_sequence(parts):
    rows, cols = lax.axis_size("row"), lax.axis_size("col")
    if not is_small(rows, cols):
        return lax.psum_scatter(parts, "col", scatter_dimension=0, tiled=True).astype(F32)
    col = lax.axis_index("col")
    count = parts.shape[0] // cols
    total = None
    for step in range(cols):
        place = (col - step + cols) % cols * count
        piece = lax.dynamic_slice_in_dim(parts, place, count, 0)
        if step:
            piece = shift_col(piece, cols - step)
        total = piece.astype(F32) if total is None else total + piece.astype(F32)
    return total


def score_tile(query, key, diagonal, mask):
    tokens, length = query.shape[0], key.shape[0]
    width = diagonal.shape[-1]
    spread = jnp.broadcast_to(diagonal, (tokens, width))
    bias = pltpu.roll(spread, 0, 1, stride=1, stride_axis=0)[:, :length]
    raw = lax.dot_general(query, key, (((1,), (1,)), ((), ())), preferred_element_type=F32)
    return raw + bias + mask


def attention_fwd_kernel(q_ref, k_ref, v_ref, diag_ref, mask_ref, out_ref, lse_ref):
    mask = mask_ref[...]
    for sub in range(2):
        lanes = slice(sub * HEAD_DIM, (sub + 1) * HEAD_DIM)
        scores = score_tile(
            q_ref[:, lanes] * BF(HEAD_DIM**-0.5), k_ref[:, lanes], diag_ref[0, sub : sub + 1], mask
        )
        maxima = jnp.max(scores, axis=-1, keepdims=True)
        weights = jnp.exp(scores - maxima)
        totals = jnp.sum(weights, axis=-1, keepdims=True)
        probability = (weights * (1.0 / totals)).astype(BF)
        out = jnp.dot(probability, v_ref[:, lanes], preferred_element_type=F32)
        out_ref[:, lanes] = out.astype(BF)
        lse_ref[:, lanes] = jnp.broadcast_to(maxima + jnp.log(totals), out.shape)


def attention_forward(q, key, value, diagonals, mask):
    tokens, width = q.shape
    length = key.shape[0]
    pairs = width // LANES
    return pl.pallas_call(
        attention_fwd_kernel,
        grid=(pairs,),
        in_specs=[
            pl.BlockSpec((tokens, LANES), lambda i: (0, i)),
            pl.BlockSpec((length, LANES), lambda i: (0, i)),
            pl.BlockSpec((length, LANES), lambda i: (0, i)),
            pl.BlockSpec((1, 2, diagonals.shape[-1]), lambda i: (i, 0, 0)),
            pl.BlockSpec((tokens, length), lambda i: (0, 0)),
        ],
        out_specs=[
            pl.BlockSpec((tokens, LANES), lambda i: (0, i)),
            pl.BlockSpec((tokens, LANES), lambda i: (0, i)),
        ],
        out_shape=[
            jax.ShapeDtypeStruct((tokens, width), BF),
            jax.ShapeDtypeStruct((tokens, width), F32),
        ],
        compiler_params=pltpu.CompilerParams(vmem_limit_bytes=VMEM_LIMIT),
        cost_estimate=pl.CostEstimate(
            flops=4 * tokens * length * width,
            bytes_accessed=8 * length * width,
            transcendentals=HEADS * tokens * length,
        ),
        name="attention_forward",
    )(q, key, value, diagonals, mask)


def attention_bwd_kernel(
    q_ref, k_ref, v_ref, ga_ref, lse_ref, diag_ref, mask_ref, dq_ref, dk_ref, dv_ref, dist_ref
):
    mask = mask_ref[...]
    tokens, length = mask.shape
    width = diag_ref.shape[-1]
    for sub in range(2):
        lanes = slice(sub * HEAD_DIM, (sub + 1) * HEAD_DIM)
        query = q_ref[:, lanes] * BF(HEAD_DIM**-0.5)
        key = k_ref[:, lanes]
        grad = ga_ref[:, lanes]
        scores = score_tile(query, key, diag_ref[0, sub : sub + 1], mask)
        lse = lse_ref[:, sub * HEAD_DIM : sub * HEAD_DIM + 1]
        probability = jnp.exp(scores - lse)
        dv = lax.dot_general(
            probability.astype(BF), grad, (((0,), (0,)), ((), ())), preferred_element_type=F32
        )
        dv_ref[:, lanes] = dv.astype(BF)
        grad_prob = lax.dot_general(
            grad, v_ref[:, lanes], (((1,), (1,)), ((), ())), preferred_element_type=F32
        )
        product = probability * grad_prob
        inner = jnp.sum(product, axis=-1, keepdims=True)
        grad_scores = product - probability * inner
        low = grad_scores.astype(BF)
        dq = jnp.dot(low, key, preferred_element_type=F32) * HEAD_DIM**-0.5
        dq_ref[:, lanes] = dq.astype(BF)
        dk = lax.dot_general(low, query, (((0,), (0,)), ((), ())), preferred_element_type=F32)
        dk_ref[:, lanes] = dk.astype(BF)
        turned = jnp.concatenate(
            [grad_scores, jnp.zeros((tokens, width - length), F32)], axis=1
        )
        half = tokens // 2
        while half >= 8:
            turned = turned[:half] + pltpu.roll(turned[half:], width - half, 1)
            half //= 2
        dist_ref[0, sub] = turned


def attention_backward(q, key, value, grad, lse, diagonals, mask):
    tokens, width = q.shape
    length = key.shape[0]
    pairs = width // LANES
    wide = diagonals.shape[-1]
    return pl.pallas_call(
        attention_bwd_kernel,
        grid=(pairs,),
        in_specs=[
            pl.BlockSpec((tokens, LANES), lambda i: (0, i)),
            pl.BlockSpec((length, LANES), lambda i: (0, i)),
            pl.BlockSpec((length, LANES), lambda i: (0, i)),
            pl.BlockSpec((tokens, LANES), lambda i: (0, i)),
            pl.BlockSpec((tokens, LANES), lambda i: (0, i)),
            pl.BlockSpec((1, 2, wide), lambda i: (i, 0, 0)),
            pl.BlockSpec((tokens, length), lambda i: (0, 0)),
        ],
        out_specs=[
            pl.BlockSpec((tokens, LANES), lambda i: (0, i)),
            pl.BlockSpec((length, LANES), lambda i: (0, i)),
            pl.BlockSpec((length, LANES), lambda i: (0, i)),
            pl.BlockSpec((1, 2, 8, wide), lambda i: (i, 0, 0, 0)),
        ],
        out_shape=[
            jax.ShapeDtypeStruct((tokens, width), BF),
            jax.ShapeDtypeStruct((length, width), BF),
            jax.ShapeDtypeStruct((length, width), BF),
            jax.ShapeDtypeStruct((pairs, 2, 8, wide), F32),
        ],
        compiler_params=pltpu.CompilerParams(vmem_limit_bytes=VMEM_LIMIT),
        cost_estimate=pl.CostEstimate(
            flops=10 * tokens * length * width,
            bytes_accessed=12 * length * width,
            transcendentals=HEADS * tokens * length,
        ),
        name="attention_backward",
    )(q, key, value, grad, lse, diagonals, mask)


def weight_copies(own, other, buffer, sem, expert, slot):
    return (
        pltpu.make_async_copy(own.at[expert], buffer.at[slot], sem.at[slot]),
        pltpu.make_async_copy(other.at[expert], buffer.at[slot], sem.at[slot]),
    )


def start_weights(own_flag, refs, expert, slot):
    for own, other, buffer, sem in refs:

        @pl.when(own_flag)
        def _():
            weight_copies(own, other, buffer, sem, expert, slot)[0].start()

        @pl.when(jnp.logical_not(own_flag))
        def _():
            weight_copies(own, other, buffer, sem, expert, slot)[1].start()


def wait_weights(refs, expert, slot):
    for own, _, buffer, sem in refs:
        pltpu.make_async_copy(own.at[expert], buffer.at[slot], sem.at[slot]).wait()


def split_two(value):
    high = value.astype(BF)
    return high, (value - high.astype(F32)).astype(BF)


def buffer_places(buffer, slot):
    half = buffer.shape[-1] // 2
    return (
        buffer.at[slot, 0],
        buffer.at[slot, 1],
        buffer.at[slot, 2],
        buffer.at[slot, 3, :, pl.ds(0, half)],
        buffer.at[slot, 3, :, pl.ds(half, half)],
    )


class Feed:
    def __init__(self, value):
        self.grouped = isinstance(value, list)
        self.arrays = [part for group in value for part in group] if self.grouped else [value]
        self.tokens, self.width = self.arrays[0].shape[-2:]

    def specs(self, group, index_map):
        if self.grouped:
            return [pl.BlockSpec(memory_space=pl.ANY)] * len(self.arrays)
        return [pl.BlockSpec((group, self.tokens, self.width), index_map)]

    def scratch(self):
        if not self.grouped:
            return []
        return [pltpu.VMEM((2, 4, self.tokens, self.width), BF), pltpu.SemaphoreType.DMA((2, 5))]


def feed_copies(refs, scratch, step, slot):
    buffer, sem = scratch
    return [
        pltpu.make_async_copy(refs[5 * step + k], place, sem.at[slot, k])
        for k, place in enumerate(buffer_places(buffer, slot))
    ]


def start_feed(refs, scratch, step, slot):
    for at in range(len(refs) // 5):

        @pl.when(step == at)
        def _():
            for copy in feed_copies(refs, scratch, at, slot):
                copy.start()


def take_feed(refs, scratch, step):
    if not scratch:
        return [refs[0][g] for g in range(refs[0].shape[0])]
    slot = lax.rem(step, 2)
    for copy in feed_copies(refs, scratch, 0, slot):
        copy.wait()
    return [scratch[0][slot, g] for g in range(4)]


def refill_feed(refs, scratch, step):
    if scratch:
        start_feed(refs, scratch, step + 2, lax.rem(step, 2))


def open_feed(refs, scratch):
    if scratch:
        start_feed(refs, scratch, 0, 0)
        start_feed(refs, scratch, 1, 1)


def sink_copies(refs, scratch, step, slot):
    buffer, sem = scratch
    return [
        pltpu.make_async_copy(place, refs[5 * step + k], sem.at[slot, k])
        for k, place in enumerate(buffer_places(buffer, slot))
    ]


def put_sink(refs, scratch, step, values):
    if not scratch:
        for g, value in enumerate(values):
            refs[0][g] = value
        return
    slot = lax.rem(step, 2)

    @pl.when(step >= 2)
    def _():
        for copy in sink_copies(refs, scratch, 0, slot):
            copy.wait()

    for g, value in enumerate(values):
        scratch[0][slot, g] = value
    for at in range(len(refs) // 5):

        @pl.when(step == at)
        def _():
            for copy in sink_copies(refs, scratch, at, slot):
                copy.start()


def close_sink(refs, scratch, steps):
    if scratch:
        for step in range(max(steps - 2, 0), steps):
            for copy in sink_copies(refs, scratch, 0, step % 2):
                copy.wait()


def sink_specs(grouped, blocks, group, rows, width, index_map):
    if not grouped:
        return (
            [pl.BlockSpec((group, rows, width), index_map)],
            [jax.ShapeDtypeStruct((blocks, rows, width), BF)],
            [],
        )
    shapes = []
    for _ in range(blocks // 4):
        shapes += [jax.ShapeDtypeStruct((rows, width), BF)] * 3
        shapes += [jax.ShapeDtypeStruct((rows, width // 2), BF)] * 2
    return (
        [pl.BlockSpec(memory_space=pl.ANY)] * len(shapes),
        shapes,
        [pltpu.VMEM((2, 4, rows, width), BF), pltpu.SemaphoreType.DMA((2, 5))],
    )


def regroup(values):
    return [tuple(values[5 * k : 5 * k + 5]) for k in range(len(values) // 5)] if len(values) > 1 else values[0]


def spread_slots(table, rows):
    return lax.dot_general(table, rows, (((0,), (0,)), ((), ())), preferred_element_type=F32)


def expert_fwd_kernel(section, group, steps, experts, counts, *refs):
    n_feed, n_sink, n_feed_scratch, n_sink_scratch = counts
    pipe_ref, refs = refs[0], refs[1:]
    feed, refs = refs[:n_feed], refs[n_feed:]
    tab_ref, named_ref, pick_ref, router_ref, own_in, oth_in, own_out, oth_out = refs[:8]
    refs = refs[8:]
    sink, refs = refs[:n_sink], refs[n_sink:]
    rows_ref, gate_ref, held, gates, buf_in, buf_out, sem_in, sem_out = refs[:8]
    refs = refs[8:]
    feed_scratch, sink_scratch = refs[:n_feed_scratch], refs[n_feed_scratch:]
    i = pl.program_id(0)
    own_flag = pipe_ref[0] == section
    weights = ((own_in, oth_in, buf_in, sem_in), (own_out, oth_out, buf_out, sem_out))
    blocks, local, places, width = held.shape
    slots = local * places

    @pl.when(i == 0)
    def _():
        open_feed(feed, feed_scratch)
        start_weights(own_flag, weights, 0, 0)
        if experts > 1:
            start_weights(own_flag, weights, 1, 1)

    @pl.when(i < steps)
    def _():
        values = take_feed(feed, feed_scratch, i)
        for g, tokens in enumerate(values):
            table = tab_ref[g]
            logits = jnp.dot(tokens, router_ref[...], preferred_element_type=F32)
            logits = jnp.where(named_ref[g].astype(F32) > 0, logits, MASKED)
            chosen = jnp.exp(logits - jnp.max(logits, axis=-1, keepdims=True))
            chosen = chosen / jnp.sum(chosen, axis=-1, keepdims=True)
            high, low = split_two(chosen)
            spread = jnp.dot(
                table, jnp.concatenate([high, low], axis=1), preferred_element_type=F32
            )
            spread = (spread[:, :LANES] + spread[:, LANES:]) * pick_ref[...]
            gate = jnp.broadcast_to(jnp.sum(spread, axis=-1, keepdims=True), (slots, LANES))
            rows = jnp.dot(table, tokens, preferred_element_type=F32).astype(BF)
            rows_ref[g] = rows.reshape(local, places, width)
            gate_ref[g] = gate.reshape(local, places, LANES)
            held[i * group + g] = rows.reshape(local, places, width)
            gates[i * group + g] = gate.reshape(local, places, LANES)
        refill_feed(feed, feed_scratch, i)

    @pl.when((i >= steps) & (i < steps + experts))
    def _():
        expert = i - steps
        slot = lax.rem(expert, 2)
        wait_weights(weights, expert, slot)
        part = blocks // 2 if blocks % 2 == 0 else blocks
        for start in range(0, blocks, part):
            some = pl.ds(start, part)
            rows = held[some, expert].reshape(part * places, width)
            hidden = jnp.dot(rows, buf_in[slot], preferred_element_type=F32)
            bent = jnp.tanh(GELU_C * (hidden + GELU_A * hidden * hidden * hidden))
            active = (0.5 * hidden * (1.0 + bent)).astype(BF)
            result = jnp.dot(active, buf_out[slot], preferred_element_type=F32)
            gate = gates[some, expert].reshape(part * places, LANES)[:, :1]
            held[some, expert] = (result * gate).astype(BF).reshape(part, places, width)

        @pl.when(expert + 2 < experts)
        def _():
            start_weights(own_flag, weights, expert + 2, slot)

    @pl.when(i >= steps + experts)
    def _():
        step = i - steps - experts
        values = [
            spread_slots(tab_ref[g], held[step * group + g].reshape(slots, width)).astype(BF)
            for g in range(group)
        ]
        put_sink(sink, sink_scratch, step, values)

    @pl.when(i == 2 * steps + experts - 1)
    def _():
        close_sink(sink, sink_scratch, steps)


def group_of(blocks):
    return 4 if blocks % 4 == 0 else 1


def grid_maps(steps, experts):
    def early(i, *_):
        return (jnp.minimum(i, steps - 1), 0, 0)

    def early4(i, *_):
        return (jnp.minimum(i, steps - 1), 0, 0, 0)

    def both(i, *_):
        return (jnp.where(i < steps + experts, jnp.minimum(i, steps - 1), i - steps - experts), 0, 0)

    def late(i, *_):
        return (jnp.maximum(i - steps - experts, 0), 0, 0)

    def per_expert(i, *_):
        return (0, jnp.clip(i - steps, 0, experts - 1), 0, 0)

    return early, early4, both, late, per_expert


def expert_forward(section, pipe, tables, tokens, named, pick, router, weights):
    own_in, oth_in, own_out, oth_out = weights
    blocks, slots, count = tables.shape
    feed = Feed(tokens)
    width = feed.width
    experts, _, hidden = own_in.shape
    places = slots // experts
    group = group_of(blocks)
    steps = blocks // group
    early, early4, both, late, _ = grid_maps(steps, experts)
    any_spec = pl.BlockSpec(memory_space=pl.ANY)
    sink_out, sink_shapes, sink_scratch = sink_specs(feed.grouped, blocks, group, count, width, late)
    feed_scratch = feed.scratch()
    counts = (len(feed.arrays), len(sink_out), len(feed_scratch), len(sink_scratch))
    *parts, rows, gates = pl.pallas_call(
        functools.partial(expert_fwd_kernel, section, group, steps, experts, counts),
        grid_spec=pltpu.PrefetchScalarGridSpec(
            num_scalar_prefetch=1,
            grid=(2 * steps + experts,),
            in_specs=feed.specs(group, early)
            + [
                pl.BlockSpec((group, slots, count), both),
                pl.BlockSpec((group, count, LANES), early),
                pl.BlockSpec((slots, LANES), lambda i, *_: (0, 0)),
                pl.BlockSpec((width, LANES), lambda i, *_: (0, 0)),
            ]
            + [any_spec] * 4,
            out_specs=sink_out
            + [
                pl.BlockSpec((group, experts, places, width), early4),
                pl.BlockSpec((group, experts, places, LANES), early4),
            ],
            scratch_shapes=[
                pltpu.VMEM((blocks, experts, places, width), BF),
                pltpu.VMEM((blocks, experts, places, LANES), F32),
                pltpu.VMEM((2, width, hidden), BF),
                pltpu.VMEM((2, hidden, width), BF),
                pltpu.SemaphoreType.DMA((2,)),
                pltpu.SemaphoreType.DMA((2,)),
            ]
            + feed_scratch
            + sink_scratch,
        ),
        out_shape=sink_shapes
        + [
            jax.ShapeDtypeStruct((blocks, experts, places, width), BF),
            jax.ShapeDtypeStruct((blocks, experts, places, LANES), F32),
        ],
        compiler_params=pltpu.CompilerParams(vmem_limit_bytes=VMEM_LIMIT),
        cost_estimate=pl.CostEstimate(
            flops=4 * blocks * slots * width * hidden,
            bytes_accessed=4 * experts * width * hidden + 8 * blocks * count * width,
            transcendentals=blocks * slots * hidden,
        ),
        name="expert_forward",
    )(pipe, *feed.arrays, tables, named, pick, router, own_in, oth_in, own_out, oth_out)
    return regroup(parts), rows, gates


def expert_bwd_kernel(section, group, steps, experts, counts, *refs):
    n_feed, n_sink, n_feed_scratch, n_sink_scratch, n_alias = counts
    pipe_ref, refs = refs[0], refs[1:]
    feed, refs = refs[:n_feed], refs[n_feed:]
    tab_ref, rows_ref, gate_ref, lane_ref, own_in, oth_in, own_out, oth_out = refs[:8]
    refs = refs[8 + n_alias :]
    sink, refs = refs[:n_sink], refs[n_sink:]
    kept_in, kept_out, sent_in, sent_out = refs[:4]
    refs = refs[4:]
    held, marks, buf_in, buf_out, grad_in, grad_out, sem_in, sem_out, sem_grad = refs[:9]
    refs = refs[9:]
    feed_scratch, sink_scratch = refs[:n_feed_scratch], refs[n_feed_scratch:]
    i = pl.program_id(0)
    own_flag = pipe_ref[0] == section
    weights = ((own_in, oth_in, buf_in, sem_in), (own_out, oth_out, buf_out, sem_out))
    blocks, local, places, width = held.shape
    slots = local * places

    def grad_copies(keep, expert, slot):
        target_in, target_out = (kept_in, kept_out) if keep else (sent_in, sent_out)
        return (
            pltpu.make_async_copy(grad_in.at[slot], target_in.at[expert], sem_grad.at[0, slot]),
            pltpu.make_async_copy(grad_out.at[slot], target_out.at[expert], sem_grad.at[1, slot]),
        )

    def wait_grads(expert, slot):
        for copy in grad_copies(True, expert, slot):
            copy.wait()

    @pl.when(i == 0)
    def _():
        open_feed(feed, feed_scratch)
        start_weights(own_flag, weights, 0, 0)
        if experts > 1:
            start_weights(own_flag, weights, 1, 1)

    @pl.when(i < steps)
    def _():
        for g, tokens in enumerate(take_feed(feed, feed_scratch, i)):
            rows = jnp.dot(tab_ref[g], tokens, preferred_element_type=F32).astype(BF)
            held[i * group + g] = rows.reshape(local, places, width)
        refill_feed(feed, feed_scratch, i)

    @pl.when((i >= steps) & (i < steps + experts))
    def _():
        expert = i - steps
        slot = lax.rem(expert, 2)
        count = blocks * places
        wait_weights(weights, expert, slot)

        @pl.when(expert >= 2)
        def _():
            wait_grads(expert, slot)

        rows = rows_ref[...].reshape(count, width)
        gate = gate_ref[...].reshape(count, LANES)[:, :1]
        grad = held[:, expert].reshape(count, width)
        hidden = jnp.dot(rows, buf_in[slot], preferred_element_type=F32)
        square = hidden * hidden
        bent = jnp.tanh(GELU_C * (hidden + GELU_A * square * hidden))
        active = (0.5 * hidden * (1.0 + bent)).astype(BF)
        slope = 0.5 * (1.0 + bent) + (0.5 * GELU_C) * hidden * (1.0 - bent * bent) * (
            1.0 + (3.0 * GELU_A) * square
        )
        grad_act = lax.dot_general(
            grad, buf_out[slot], (((1,), (1,)), ((), ())), preferred_element_type=F32
        )
        mark = jnp.sum(active.astype(F32) * grad_act, axis=-1, keepdims=True)
        first = mark.astype(BF).astype(F32)
        lanes = lane_ref[...].reshape(count, LANES).astype(F32)
        which = lax.rem(lax.broadcasted_iota(jnp.int32, (count, LANES), 1), 8)
        value = jnp.where(which == 0, first, mark - first)
        marks[:, expert] = (value * lanes).astype(BF).reshape(blocks, places, LANES)
        gated = (grad.astype(F32) * gate).astype(BF)
        grad_out[slot] = spread_slots(active, gated).astype(BF)
        grad_hidden = (grad_act * gate * slope).astype(BF)
        grad_in[slot] = spread_slots(rows, grad_hidden).astype(BF)
        back = lax.dot_general(
            grad_hidden, buf_in[slot], (((1,), (1,)), ((), ())), preferred_element_type=F32
        )
        held[:, expert] = back.astype(BF).reshape(blocks, places, width)

        @pl.when(own_flag)
        def _():
            for copy in grad_copies(True, expert, slot):
                copy.start()

        @pl.when(jnp.logical_not(own_flag))
        def _():
            for copy in grad_copies(False, expert, slot):
                copy.start()

        @pl.when(expert + 2 < experts)
        def _():
            start_weights(own_flag, weights, expert + 2, slot)

    @pl.when(i >= steps + experts)
    def _():
        step = i - steps - experts
        values = []
        for g in range(group):
            place = step * group + g
            table = tab_ref[g]
            rows = spread_slots(table, held[place].reshape(slots, width))
            found = spread_slots(marks[place].reshape(slots, LANES), table)
            count = found.shape[1]
            line = jnp.concatenate(
                [
                    jnp.sum(found[0:8], axis=0, keepdims=True),
                    jnp.sum(found[8:16], axis=0, keepdims=True),
                    jnp.zeros((1, width - 2 * count), F32),
                ],
                axis=1,
            )
            values.append(
                jnp.concatenate(
                    [rows.astype(BF), jnp.broadcast_to(line, (SCORE_ROWS, width)).astype(BF)], axis=0
                )
            )
        put_sink(sink, sink_scratch, step, values)

    @pl.when(i == 2 * steps + experts - 1)
    def _():
        close_sink(sink, sink_scratch, steps)
        for expert in range(max(experts - 2, 0), experts):
            wait_grads(expert, expert % 2)


def expert_backward(section, pipe, tables, grads, rows, gates, lanes, weights, stores):
    own_in, oth_in, own_out, oth_out = weights
    blocks, slots, count = tables.shape
    feed = Feed(grads)
    width = feed.width
    experts, _, hidden = own_in.shape
    places = slots // experts
    group = group_of(blocks)
    steps = blocks // group
    early, _, both, late, per_expert = grid_maps(steps, experts)
    any_spec = pl.BlockSpec(memory_space=pl.ANY)
    sink_out, sink_shapes, sink_scratch = sink_specs(
        feed.grouped, blocks, group, count + SCORE_ROWS, width, late
    )
    feed_scratch = feed.scratch()
    shape_in = jax.ShapeDtypeStruct(own_in.shape, BF)
    shape_out = jax.ShapeDtypeStruct(own_out.shape, BF)
    operands = [pipe, *feed.arrays, tables, rows, gates, lanes, own_in, oth_in, own_out, oth_out]
    aliases = {}
    if stores is not None:
        aliases = {len(operands) + k: len(sink_out) + k for k in range(4)}
        operands += list(stores)
    counts = (len(feed.arrays), len(sink_out), len(feed_scratch), len(sink_scratch), len(aliases))
    outs = pl.pallas_call(
        functools.partial(expert_bwd_kernel, section, group, steps, experts, counts),
        grid_spec=pltpu.PrefetchScalarGridSpec(
            num_scalar_prefetch=1,
            grid=(2 * steps + experts,),
            in_specs=feed.specs(group, early)
            + [
                pl.BlockSpec((group, slots, count), both),
                pl.BlockSpec((blocks, 1, places, width), per_expert),
                pl.BlockSpec((blocks, 1, places, LANES), per_expert),
                pl.BlockSpec((blocks, 1, places, LANES), per_expert),
            ]
            + [any_spec] * (4 + len(aliases)),
            out_specs=sink_out + [any_spec] * 4,
            scratch_shapes=[
                pltpu.VMEM((blocks, experts, places, width), BF),
                pltpu.VMEM((blocks, experts, places, LANES), BF),
                pltpu.VMEM((2, width, hidden), BF),
                pltpu.VMEM((2, hidden, width), BF),
                pltpu.VMEM((2, width, hidden), BF),
                pltpu.VMEM((2, hidden, width), BF),
                pltpu.SemaphoreType.DMA((2,)),
                pltpu.SemaphoreType.DMA((2,)),
                pltpu.SemaphoreType.DMA((2, 2)),
            ]
            + feed_scratch
            + sink_scratch,
        ),
        out_shape=sink_shapes + [shape_in, shape_out, shape_in, shape_out],
        input_output_aliases=aliases,
        compiler_params=pltpu.CompilerParams(vmem_limit_bytes=VMEM_LIMIT),
        cost_estimate=pl.CostEstimate(
            flops=10 * blocks * slots * width * hidden,
            bytes_accessed=8 * experts * width * hidden + 8 * blocks * count * width,
            transcendentals=blocks * slots * hidden,
        ),
        name="expert_backward",
    )(*operands)
    return regroup(outs[: len(sink_out)]), outs[len(sink_out) :]


def dense_kernel(normed_ref, seq_ref, att_ref, dq_ref, dk_ref, dv_ref, branch_ref, out_ref):
    quarter = pl.program_id(0) // 3

    def product(left, right):
        out_ref[...] = spread_slots(left[...], right[...]).astype(BF)

    pl.when(quarter == 0)(lambda: product(normed_ref, dq_ref))
    pl.when(quarter == 1)(lambda: product(seq_ref, dk_ref))
    pl.when(quarter == 2)(lambda: product(seq_ref, dv_ref))
    pl.when(quarter == 3)(lambda: product(att_ref, branch_ref))


def dense_grads(normed, sequence, attended, dq, dk, dv, branch):
    tokens, width = normed.shape
    length = sequence.shape[0]
    third = width // 3

    def whole(rows):
        return pl.BlockSpec((rows, width), lambda i: (0, 0))

    def block(rows, quarter):
        return pl.BlockSpec((rows, third), lambda i: (0, jnp.clip(i - 3 * quarter, 0, 2)))

    return pl.pallas_call(
        dense_kernel,
        grid=(12,),
        in_specs=[
            whole(tokens), whole(length), whole(tokens),
            block(tokens, 0), block(length, 1), block(length, 2), block(tokens, 3),
        ],
        out_specs=pl.BlockSpec((width, third), lambda i: (0, i)),
        out_shape=jax.ShapeDtypeStruct((width, 4 * width), BF),
        compiler_params=pltpu.CompilerParams(vmem_limit_bytes=VMEM_LIMIT),
        cost_estimate=pl.CostEstimate(
            flops=4 * width * width * (tokens + length),
            bytes_accessed=8 * length * width + 8 * width * width,
            transcendentals=0,
        ),
        name="dense_grads",
    )(normed, sequence, attended, dq, dk, dv, branch)


def slot_tables(named_by, first_expert, local_experts, places):
    tokens = named_by.shape[-1]
    ids = first_expert + jnp.arange(local_experts, dtype=jnp.int32)
    hot = [named_by[:, k, None, :] == ids[None, :, None] for k in range(TOP)]
    before = (
        jnp.arange(tokens, dtype=jnp.int32)[:, None] < jnp.arange(tokens, dtype=jnp.int32)[None, :]
    ).astype(BF)
    code = jnp.full(hot[0].shape, -1, jnp.int32)
    earlier = jnp.zeros(hot[0].shape[:2] + (1,), F32)
    for k in range(TOP):
        ones = hot[k].astype(BF)
        running = jnp.einsum("bet,tu->beu", ones, before, preferred_element_type=F32) + earlier
        code = jnp.where(hot[k], running.astype(jnp.int32), code)
        earlier = earlier + jnp.sum(ones.astype(F32), axis=-1, keepdims=True)
    place = jnp.arange(places, dtype=jnp.int32)
    equal = code[:, :, None, :] == place[None, None, :, None]
    tables = equal.astype(BF)
    second = jnp.max(jnp.where(equal & hot[1][:, :, None, :], 1.0, 0.0), axis=-1)
    lane = jnp.arange(LANES, dtype=jnp.int32)
    wanted = jnp.where(second[..., None] > 0.5, (lane >= 8) & (lane < 11), lane < 3)
    blocks = named_by.shape[0]
    return tables.reshape(blocks, local_experts * places, tokens), wanted.astype(BF)


def named_mask(named_by):
    lane = jnp.arange(LANES, dtype=jnp.int32)
    hit = named_by[:, 0, :, None] == lane
    for k in range(1, TOP):
        hit = hit | (named_by[:, k, :, None] == lane)
    return hit.astype(BF)


def on_device(
    section_input,
    cotangent,
    qkv_weight,
    out_weight,
    router_weight,
    gain_attn,
    gain_moe,
    rel_bias,
    expert_in,
    expert_out,
    routes,
    doc_ids,
    buckets,
):
    pipe = lax.axis_index("pipe")
    row, col = lax.axis_index("row"), lax.axis_index("col")
    row_count, col_count = lax.axis_size("row"), lax.axis_size("col")
    group_size = row_count * col_count
    tokens, width = section_input.shape[1:]
    length = buckets.shape[0]
    capacity = 3 * tokens * TOP // (2 * EXPERTS)
    places = -(-capacity // 16) * 16
    local_experts = expert_in.shape[1]
    first = pipe == 0
    pipe_word = pipe.astype(jnp.int32)[None]
    order = block_order(row_count, col_count)

    shard = qkv_weight.shape[1]
    bias_count = rel_bias.shape[1]
    middle = 2 * width

    def line(values):
        flat = jnp.concatenate([value.reshape(-1) for value in values])
        return jnp.pad(flat, (0, 2 * middle - flat.shape[0])).reshape(2, middle)

    small = jnp.concatenate(
        [
            line([router_weight[0]]),
            line([gain_attn[0], gain_moe[0], rel_bias[0]]),
            line([jnp.swapaxes(routes[0], 1, 2).astype(BF)]),
            jnp.zeros((SMALL_ROWS - 6, middle), BF),
        ],
        axis=0,
    )
    left = qkv_weight[0][:, :middle]
    right = jnp.concatenate([qkv_weight[0][:, middle:], out_weight[0]], axis=1)
    swapped = swap_pipe(jnp.where(first, right, left))
    mine = [jnp.where(first, left, swapped), jnp.where(first, swapped, right)]
    whole = gather_absolute(jnp.concatenate([mine[0], small], axis=0), order)
    whole = lax.optimization_barrier(whole)
    partner = swap_pipe(whole)
    later, _ = lax.optimization_barrier((mine[1], whole))
    later = lax.all_gather(later, ("row", "col"), axis=0)
    later_partner = swap_pipe(later)
    expert_first, expert_second, _ = lax.optimization_barrier((expert_in[0], expert_out[0], swapped))
    expert_weights = (expert_first, swap_pipe(expert_first), expert_second, swap_pipe(expert_second))
    halves = [
        [jnp.where(first, whole[:, :shard], partner[:, :shard]), jnp.where(first, partner[:, :shard], whole[:, :shard])],
        [jnp.where(first, later, later_partner), jnp.where(first, later_partner, later)],
    ]
    smalls = [
        jnp.where(first, whole[:, shard:], partner[:, shard:]),
        jnp.where(first, partner[:, shard:], whole[:, shard:]),
    ]
    params = []
    names = []
    for section in range(2):
        lines = smalls[section].reshape(group_size, SMALL_ROWS // 2, 2 * middle)
        low, high = [value.reshape(width, middle) for value in halves[section]]
        router = lines[:, 0, : shard * EXPERTS].reshape(width, EXPERTS)
        params.append(
            dict(
                q=low[:, :width],
                k=low[:, width:],
                v=high[:, :width],
                out=high[:, width:],
                router=jnp.pad(router, ((0, 0), (0, LANES - EXPERTS))),
                gain_attn=lines[:, 1, :shard].reshape(width).astype(F32),
                gain_moe=lines[:, 1, shard : 2 * shard].reshape(width).astype(F32),
                table=lines[:, 1, 2 * shard : 2 * shard + bias_count].reshape(NBUCKET, HEADS),
            )
        )
        named_by = lines[:, 2, : 2 * TOP * tokens].reshape(group_size, 2, TOP, tokens)
        named_by = lax.dynamic_index_in_dim(named_by, pipe, 1, keepdims=False)
        names.append(named_by.astype(jnp.int32))

    first_expert = row * local_experts
    tables, lane_masks, named = [], [], []
    for section in range(2):
        placed = jnp.take(names[section], order, axis=0)
        table, wanted = slot_tables(placed, first_expert, local_experts, places)
        tables.append(table)
        lane_masks.append(wanted)
        named.append(named_mask(placed))
    home = [
        lax.dynamic_index_in_dim(value, row * col_count + col, 0, keepdims=False).T for value in names
    ]
    slots = local_experts * places
    pick = (
        jnp.arange(LANES, dtype=jnp.int32)[None, :]
        == (first_expert + jnp.arange(slots, dtype=jnp.int32) // places)[:, None]
    ).astype(F32)

    offset = col * tokens
    docs = lax.dynamic_index_in_dim(doc_ids, pipe, 0, keepdims=False)
    doc_query = lax.dynamic_slice_in_dim(docs, offset, tokens, 0)
    query_place = offset + jnp.arange(tokens, dtype=jnp.int32)
    allowed = (query_place[:, None] >= jnp.arange(length, dtype=jnp.int32)[None, :]) & (
        doc_query[:, None] == docs[None, :]
    )
    mask = jnp.where(allowed, 0.0, MASKED).astype(F32)
    falling = jnp.concatenate(
        [buckets[-1:], jnp.flip(buckets), jnp.zeros((length,), jnp.int32)], axis=0
    )
    by_place = jnp.concatenate(
        [
            lax.dynamic_slice_in_dim(falling, length - offset, length, 0),
            lax.dynamic_slice_in_dim(falling, length - offset - tokens, tokens, 0),
        ],
        axis=0,
    )
    bucket_hot = jnp.arange(NBUCKET, dtype=jnp.int32)[:, None] == by_place[None, :]
    diagonals = [
        jnp.einsum(
            "bh,bx->hx", value["table"], bucket_hot.astype(BF), preferred_element_type=F32
        ).reshape(HEADS // 2, 2, -1)
        for value in params
    ]

    stream = lax.dynamic_index_in_dim(section_input, pipe, 0, keepdims=False)
    results = []
    kept = []
    for section in range(2):
        weight = params[section]
        normed_attn = norm_scale(stream, weight["gain_attn"]).astype(BF)
        sequence = gather_sequence(normed_attn)
        q = jnp.dot(normed_attn, weight["q"], preferred_element_type=F32).astype(BF)
        key = jnp.dot(sequence, weight["k"], preferred_element_type=F32).astype(BF)
        value = jnp.dot(sequence, weight["v"], preferred_element_type=F32).astype(BF)
        attended, lse = attention_forward(q, key, value, diagonals[section], mask)
        after_attn = stream + jnp.dot(attended, weight["out"], preferred_element_type=F32)
        normed_moe = norm_scale(after_attn, weight["gain_moe"]).astype(BF)
        part, rows, gates = expert_forward(
            section, pipe_word, tables[section], gather_tokens(normed_moe), named[section], pick,
            weight["router"], expert_weights,
        )
        result = after_attn + scatter_tokens(part)
        kept.append(
            (stream, normed_attn, sequence, q, key, value, lse, attended, after_attn, normed_moe, rows, gates)
        )
        results.append(result)
        stream = result

    grad = lax.dynamic_index_in_dim(cotangent, pipe, 0, keepdims=False)
    lane_ids = jnp.arange(LANES, dtype=jnp.int32)[None, :]
    input_grads = [None, None]
    dense = [None, None]
    stores = None
    for section in (1, 0):
        weight = params[section]
        (
            stream, normed_attn, sequence, q, key, value, lse, attended, after_attn, normed_moe, rows, gates
        ) = kept[section]
        part, stores = expert_backward(
            section, pipe_word, tables[section], gather_tokens(grad.astype(BF)), rows, gates,
            lane_masks[section], expert_weights, stores,
        )
        named_by = home[section]
        logits = jnp.dot(normed_moe, weight["router"], preferred_element_type=F32)
        chosen = jnp.stack(
            [
                jnp.sum(jnp.where(named_by[:, k : k + 1] == lane_ids, logits, 0.0), axis=1)
                for k in range(TOP)
            ],
            axis=1,
        )
        chosen = jnp.exp(chosen - jnp.max(chosen, axis=1, keepdims=True))
        gate_weights = chosen / jnp.sum(chosen, axis=1, keepdims=True)
        summed = scatter_tokens(part)
        grad_gate = summed[tokens, : TOP * tokens].reshape(TOP, tokens).T
        grad_chosen = gate_weights * (
            grad_gate - jnp.sum(gate_weights * grad_gate, axis=1, keepdims=True)
        )
        grad_logits = jnp.zeros((tokens, LANES), F32)
        for k in range(TOP):
            grad_logits = grad_logits + jnp.where(
                named_by[:, k : k + 1] == lane_ids, grad_chosen[:, k : k + 1], 0.0
            )
        grad_logits = grad_logits.astype(BF)
        grad_router = jnp.einsum("td,te->de", normed_moe, grad_logits, preferred_element_type=F32)
        grad_normed = summed[:tokens] + jnp.einsum(
            "te,de->td", grad_logits, weight["router"], preferred_element_type=F32
        )
        _, norm_back = jax.vjp(norm_scale, after_attn, weight["gain_moe"])
        grad_after, grad_gain_moe = norm_back(grad_normed)
        grad_after = grad + grad_after
        grad_branch = grad_after.astype(BF)
        grad_attended = jnp.einsum(
            "td,cd->tc", grad_branch, weight["out"], preferred_element_type=F32
        ).astype(BF)
        dq, dk, dv, dist = attention_backward(
            q, key, value, grad_attended, lse, diagonals[section], mask
        )
        partial = jnp.einsum("td,cd->tc", dk, weight["k"], preferred_element_type=F32) + jnp.einsum(
            "td,cd->tc", dv, weight["v"], preferred_element_type=F32
        )
        partial = partial.astype(BF)
        if section == 0:
            kept_in, kept_out, sent_in, sent_out = stores
            total_in = kept_in.astype(F32) + swap_pipe(sent_in).astype(F32)
            total_out = kept_out.astype(F32) + swap_pipe(sent_out).astype(F32)
        grad_normed = scatter_sequence(partial) + jnp.einsum(
            "td,cd->tc", dq, weight["q"], preferred_element_type=F32
        )
        _, norm_back = jax.vjp(norm_scale, stream, weight["gain_attn"])
        grad_stream, grad_gain_attn = norm_back(grad_normed)
        grad = grad_after + grad_stream
        input_grads[section] = grad
        dist = dist.reshape(HEADS, 8, -1)
        by_distance = dist[:, 0]
        for turn in range(1, 8):
            by_distance = by_distance + jnp.roll(dist[:, turn], -turn, axis=1)
        grad_table = jnp.einsum(
            "bx,hx->bh", bucket_hot.astype(F32), by_distance, precision=HIGH, preferred_element_type=F32
        )

        def lines(values):
            flat = jnp.concatenate([value.reshape(group_size, -1) for value in values], axis=1)
            flat = jnp.pad(flat, ((0, 0), (0, 2 * middle - flat.shape[1])))
            return flat.astype(BF)[:, None]

        small = jnp.concatenate(
            [
                lines([grad_router[:, :EXPERTS]]),
                lines([grad_gain_attn, grad_gain_moe, grad_table]),
                jnp.zeros((group_size, 6, 2 * middle), BF),
            ],
            axis=1,
        )
        large = dense_grads(normed_attn, sequence, attended, dq, dk, dv, grad_branch)
        packed = jnp.concatenate([large.reshape(group_size, shard, -1), small], axis=1)
        sent = lax.ppermute(packed, "pipe", [(1 - section, section)])
        dense[section] = packed.astype(F32) + sent.astype(F32)

    summed = scatter_absolute(jnp.where(first, dense[0], dense[1]).astype(BF), order)
    flat = summed[shard:]

    def by_micro_batch(values):
        own = jnp.where(first, values[0], values[1])
        other = swap_pipe(jnp.where(first, values[1], values[0]))
        return jnp.where(first, jnp.stack([own, other]), jnp.stack([other, own]))[None]

    return (
        by_micro_batch(results),
        by_micro_batch(input_grads),
        summed[None, :shard, : 3 * width],
        summed[None, :shard, 3 * width :],
        flat[0, : shard * EXPERTS].reshape(1, shard, EXPERTS),
        flat[1, :shard][None],
        flat[1, shard : 2 * shard][None],
        flat[1, 2 * shard : 2 * shard + bias_count][None],
        total_in[None],
        total_out[None],
    )


def solution(mesh):
    return jax.shard_map(
        on_device,
        mesh=mesh,
        in_specs=(
            P(None, ("row", "col"), None),
            P(None, ("row", "col"), None),
            P("pipe", ("row", "col"), None),
            P("pipe", ("row", "col"), None),
            P("pipe", ("row", "col"), None),
            P("pipe", ("row", "col")),
            P("pipe", ("row", "col")),
            P("pipe", ("row", "col")),
            P("pipe", "row", None, "col"),
            P("pipe", "row", "col", None),
            P("pipe", None, ("row", "col"), None),
            P(None, "row"),
            P(),
        ),
        out_specs=(
            P("pipe", None, ("row", "col"), None),
            P("pipe", None, ("row", "col"), None),
            P("pipe", ("row", "col"), None),
            P("pipe", ("row", "col"), None),
            P("pipe", ("row", "col"), None),
            P("pipe", ("row", "col")),
            P("pipe", ("row", "col")),
            P("pipe", ("row", "col")),
            P("pipe", "row", None, "col"),
            P("pipe", "row", "col", None),
        ),
        check_vma=False,
    )
```
